32 devices in a mesh: pipe: 4 (over y, core), dp: 4 (over z), tensor: 2 (over x).
Axes of the slice: x: 2, y: 2, z: 4, core: 2. Of those that a mesh axis runs over, the one named last changes fastest.
Arguments:
- tokens: bfloat16 [128, 16384], P('dp', 'tensor'), may hold values from -6 to 6
- weight: bfloat16 [4, 16384, 2, 8192], P('pipe', 'tensor', None, 'dp'), may hold values from -0.046875 to 0.046875
- gain: float32 [4, 16384], P('pipe', 'tensor'), may hold values from 0.5 to 1.5
- resident_down: bfloat16 [4, 32, 16, 16384], P('pipe', None, None, 'tensor'), may hold values from -0.046875 to 0.046875
- resident_up: bfloat16 [4, 32, 16, 16384], P('pipe', None, None, 'tensor'), may hold values from -0.23925781 to 0.23925781
- cotangent: bfloat16 [128, 16384], P('dp', 'tensor'), may hold values from -6 to 6
- batch_tenants: int32 [16], P('dp'), may hold values from 0 to 31
- tenant_slots: int32 [32], replicated, may hold values from 0 to 31, each once
Outputs:
- section_out: bfloat16 [4, 128, 16384], P('pipe', 'dp', 'tensor')
- input_grads: bfloat16 [4, 128, 16384], P('pipe', 'dp', 'tensor')
- grad_a: float32 [4, 32, 16, 16384], P('pipe', 'dp', None, 'tensor')
- grad_b: float32 [4, 32, 16, 16384], P('pipe', 'dp', None, 'tensor')
The draws below stay inside these ranges and needn't reach their ends.
All inputs are finite; a program needn't handle non-finite values.
Results may differ from the reference program's by a relative error of at most 0.018.
Values may be sent and summed in bfloat16 or wider, within the bound.
A program may use at most 384 MiB of HBM per device.

```python
import jax
import jax.numpy as jnp
from jax import lax

MODEL_WIDTH = 16384
ADAPTER_RANK = 16
TENANT_COUNT = 32
MICRO = 4
ROWS = 8
TOKENS = 128
N_PIPE = 4
N_DP = 4
N_TENSOR = 2


def touch_ends(array, key, smallest, high):
    extent = array.shape
    place = [jax.random.randint(jax.random.fold_in(key, axis), (), 0, extent[axis]) for axis in range(len(extent))]
    array = array.at[tuple(place)].set(smallest)
    longest = extent.index(max(extent))
    place[longest] = (place[longest] + 1) % extent[longest]
    return array.at[tuple(place)].set(high)


def block_levels(own_key, shape, pieces, smallest, high):
    factor_of, own = 1.0, jax.random.fold_in(own_key, 6)
    for axis_at, blocks in pieces:
        heights = jnp.exp(jax.random.uniform(jax.random.fold_in(own, axis_at), (blocks,), jnp.float32, smallest / len(pieces), high / len(pieces)))
        factor_of = factor_of * jnp.repeat(heights, shape[axis_at] // blocks).reshape([-1 if axis == axis_at else 1 for axis in range(len(shape))])
    return factor_of


def gaussian(rng, shape, width, most, cuts=(), held_as=jnp.bfloat16):
    result = jax.random.normal(rng, shape, jnp.float32) * width
    if len(cuts) > 0:
        result = block_levels(rng, shape, cuts, -0.22, 0.18) * result
    return jnp.clip(result, min=-most, max=most).astype(held_as)


def setup_inputs(seed: int = 0) -> dict:
    keys = jax.random.split(jax.random.key(seed), 9)
    return {
        "tokens": gaussian(keys[0], (TOKENS, MODEL_WIDTH), 1.0, 6.0, ((0, 4), (1, 2))),
        "weight": gaussian(keys[1], (N_PIPE, MODEL_WIDTH, N_TENSOR, MODEL_WIDTH // N_TENSOR), MODEL_WIDTH ** -0.5, 0.046875, ((0, 4), (1, 2), (3, 4))),
        "gain": jnp.clip(1.0 + 0.1 * jax.random.normal(keys[2], (N_PIPE, MODEL_WIDTH), jnp.float32), 0.5, 1.5),
        "resident_down": gaussian(keys[3], (N_PIPE, TENANT_COUNT, ADAPTER_RANK, MODEL_WIDTH), MODEL_WIDTH ** -0.5, 0.046875, ((0, 4), (3, 2))),
        "resident_up": gaussian(keys[4], (N_PIPE, TENANT_COUNT, ADAPTER_RANK, MODEL_WIDTH), 0.04, 0.23925781, ((0, 4), (3, 2))),
        "cotangent": gaussian(keys[5], (TOKENS, MODEL_WIDTH), 1.0, 6.0, ((0, 4), (1, 2))),
        "batch_tenants": touch_ends(jax.random.randint(keys[6], (N_DP * MICRO,), 0, TENANT_COUNT), jax.random.fold_in(keys[6], 1), 0, TENANT_COUNT - 1).astype(jnp.int32),
        "tenant_slots": jax.random.permutation(keys[7], TENANT_COUNT).astype(jnp.int32),
    }


EPS = 1e-05
ADAPTER_SCALE = 2.0

def reference(tokens, weight, gain, resident_down, resident_up, cotangent, batch_tenants, tenant_slots):
    block_width = MODEL_WIDTH // N_TENSOR
    tok_count = tokens.shape[0]
    slot_ids = tenant_slots[batch_tenants]
    row_slots = jnp.repeat(slot_ids, ROWS)
    labels = jnp.arange(TENANT_COUNT, dtype=jnp.int32)
    picks = (row_slots[:, None] == labels[None, :]).astype(jnp.float32)
    picks_low = picks.astype(jnp.bfloat16)
    current = tokens
    keep_list = []
    outputs = []
    for layer_index in range(N_PIPE):
        w_full = weight[layer_index].reshape(MODEL_WIDTH, MODEL_WIDTH)
        down_flattened = resident_down[layer_index].reshape(TENANT_COUNT * ADAPTER_RANK, MODEL_WIDTH)
        up_flattened = resident_up[layer_index].reshape(TENANT_COUNT * ADAPTER_RANK, MODEL_WIDTH)
        wide_state = current.astype(jnp.float32)
        inverse = lax.rsqrt(lax.optimization_barrier(jnp.mean(wide_state * wide_state, axis=1)) + EPS)
        normed_input = (wide_state * inverse[:, None] * gain[layer_index][None, :]).astype(jnp.bfloat16)
        frozen_output = jnp.zeros((tok_count, MODEL_WIDTH), jnp.float32)
        low_sum = jnp.zeros((tok_count, ADAPTER_RANK), jnp.float32)
        for block_id in range(N_TENSOR):
            first = block_id * block_width
            segment = normed_input[:, first:first + block_width]
            product = jnp.dot(segment, w_full[first:first + block_width, :], preferred_element_type=jnp.float32)
            frozen_output = frozen_output + product.astype(jnp.bfloat16).astype(jnp.float32)
            all_terms = lax.dot_general(segment, down_flattened[:, first:first + block_width], (((1,), (1,)), ((), ())), preferred_element_type=jnp.float32)
            chosen = lax.optimization_barrier(jnp.sum(all_terms.reshape(tok_count, TENANT_COUNT, ADAPTER_RANK) * picks[:, :, None], axis=1))
            low_sum = low_sum + chosen.astype(jnp.bfloat16).astype(jnp.float32)
        low_rank_state = low_sum.astype(jnp.bfloat16)
        spread_state = (picks_low[:, :, None] * low_rank_state[:, None, :]).reshape(tok_count, TENANT_COUNT * ADAPTER_RANK)
        adapter_branch = frozen_output + ADAPTER_SCALE * jnp.dot(spread_state, up_flattened, preferred_element_type=jnp.float32)
        new_state = (wide_state + adapter_branch).astype(jnp.bfloat16)
        keep_list.append((current, inverse, normed_input, spread_state, adapter_branch))
        outputs.append(new_state)
        current = new_state
    incoming_state = cotangent
    grads_in = [None] * N_PIPE
    down_gradients = [None] * N_PIPE
    up_gradients = [None] * N_PIPE
    for layer_index in range(N_PIPE - 1, -1, -1):
        current, inverse, normed_input, spread_state, adapter_branch = keep_list[layer_index]
        w_full = weight[layer_index].reshape(MODEL_WIDTH, MODEL_WIDTH)
        down_flattened = resident_down[layer_index].reshape(TENANT_COUNT * ADAPTER_RANK, MODEL_WIDTH)
        up_flattened = resident_up[layer_index].reshape(TENANT_COUNT * ADAPTER_RANK, MODEL_WIDTH)
        grad_wide = incoming_state.astype(jnp.float32)
        frozen_backward = lax.dot_general(incoming_state, w_full, (((1,), (1,)), ((), ())), preferred_element_type=jnp.float32)
        all_terms = lax.dot_general(incoming_state, up_flattened, (((1,), (1,)), ((), ())), preferred_element_type=jnp.float32)
        low_grad = lax.optimization_barrier(jnp.sum(all_terms.reshape(tok_count, TENANT_COUNT, ADAPTER_RANK) * picks[:, :, None], axis=1)).astype(jnp.bfloat16)
        spread_gradient = (picks_low[:, :, None] * low_grad[:, None, :]).reshape(tok_count, TENANT_COUNT * ADAPTER_RANK)
        statistic = lax.optimization_barrier(jnp.sum(grad_wide * adapter_branch, axis=1))
        normed_gradient = frozen_backward + ADAPTER_SCALE * jnp.dot(spread_gradient, down_flattened, preferred_element_type=jnp.float32)
        wide_state = current.astype(jnp.float32)
        change = grad_wide + inverse[:, None] * gain[layer_index][None, :] * normed_gradient - wide_state * (inverse * inverse * statistic / MODEL_WIDTH)[:, None]
        new_grad = change.astype(jnp.bfloat16)
        down_gradients[layer_index] = (ADAPTER_SCALE * jnp.dot(spread_gradient.T, normed_input, preferred_element_type=jnp.float32)).reshape(TENANT_COUNT, ADAPTER_RANK, MODEL_WIDTH)
        up_gradients[layer_index] = (ADAPTER_SCALE * jnp.dot(spread_state.T, incoming_state, preferred_element_type=jnp.float32)).reshape(TENANT_COUNT, ADAPTER_RANK, MODEL_WIDTH)
        grads_in[layer_index] = new_grad
        incoming_state = new_grad
    return (jnp.stack(outputs), jnp.stack(grads_in), jnp.stack(down_gradients), jnp.stack(up_gradients))
```

```python
import jax
import jax.numpy as jnp
from jax import lax
from jax.sharding import PartitionSpec as P

EPS = 1e-05
ADAPTER_SCALE = 2.0
F32 = jnp.float32
BF16 = jnp.bfloat16


def make_local(section_count, dp_count, tensor_count):
    axes = ("pipe", "dp", "tensor")

    def index_of(section, dp, tensor):
        return (section * dp_count + dp) * tensor_count + tensor

    def send(value, source, target, dp_shift=0, tensor_shift=0):
        pairs = [
            (
                index_of(source, d, t),
                index_of(target, (d + dp_shift) % dp_count, (t + tensor_shift) % tensor_count),
            )
            for d in range(dp_count)
            for t in range(tensor_count)
        ]
        return lax.ppermute(value, axes, pairs)

    def local(tokens, weight, gain, resident_down, resident_up, cotangent, batch_tenants, tenant_slots):
        section_id = lax.axis_index("pipe")
        dp_id = lax.axis_index("dp")
        tensor_id = lax.axis_index("tensor")
        w_block = weight[0]
        gain_row = gain[0]
        width_local, _, piece_cols = w_block.shape
        w_flat = w_block.reshape(width_local, tensor_count * piece_cols)
        model_width = width_local * tensor_count
        own_rows = tokens.shape[0]
        rows = own_rows * dp_count
        slots, rank = resident_down.shape[1:3]
        micro_rows = own_rows // batch_tenants.shape[0]
        own_slots = slots // dp_count
        down_flat = resident_down[0].reshape(slots * rank, width_local)
        up_flat = resident_up[0].reshape(slots * rank, width_local)
        first_col = dp_id * piece_cols

        def own_cols(array):
            return lax.dynamic_slice_in_dim(array, first_col, piece_cols, array.ndim - 1)

        down_cols = own_cols(down_flat)
        up_cols = own_cols(up_flat)
        gain_cols = own_cols(gain_row)
        all_tenants = lax.all_gather(batch_tenants, "dp", axis=0, tiled=True)
        labels = jnp.arange(slots, dtype=jnp.int32)
        slot_ids = jnp.sum(
            jnp.where(all_tenants[:, None] == labels[None, :], tenant_slots[None, :], 0), axis=1
        )
        row_slots = jnp.repeat(slot_ids, micro_rows)
        picks = row_slots[:, None] == labels[None, :]
        lane_slot = jnp.arange(slots * rank, dtype=jnp.int32) // rank
        lane_rank = jnp.arange(slots * rank, dtype=jnp.int32) % rank
        lane_pick = row_slots[:, None] == lane_slot[None, :]
        fold = (lane_rank[:, None] == jnp.arange(rank)[None, :]).astype(F32)
        first_lane = dp_id * own_slots * rank

        def narrow(terms):
            kept = jnp.where(lane_pick, terms, 0.0).reshape(rows, slots, rank)
            return jnp.sum(kept, axis=1).T

        def spread(values):
            wide = jnp.tile(values, (1, slots))
            return jnp.where(lane_pick, wide, jnp.zeros((), values.dtype))

        def gather_dp(parts_by_shift, axis):
            stacked = jnp.stack(parts_by_shift)
            order = [
                lax.dynamic_index_in_dim(stacked, (dp_id - d) % dp_count, 0, keepdims=False)
                for d in range(dp_count)
            ]
            return jnp.concatenate(order, axis=axis)

        def gather_tensor(parts_by_shift):
            stacked = jnp.stack(parts_by_shift)
            order = [
                lax.dynamic_index_in_dim(stacked, (tensor_id - t) % tensor_count, 0, keepdims=False)
                for t in range(tensor_count)
            ]
            return jnp.concatenate(order, axis=1)

        def sum_tensor(value, section):
            total = value
            for shift in range(1, tensor_count):
                total = total + send(value, section, section, 0, shift)
            return total

        def sum_dp(value, section):
            total = value
            for shift in range(1, dp_count):
                total = total + send(value, section, section, shift, 0)
            return total

        def dp_all(value, source, target):
            head = value if source == target else send(value, source, target)
            return [head] + [send(value, source, target, s) for s in range(1, dp_count)]

        def rows_from_cols(value, section):
            parts = []
            for shift in range(dp_count):
                at = ((dp_id + shift) % dp_count) * own_rows
                block = lax.dynamic_slice_in_dim(value, at, own_rows, 0)
                parts.append(block if shift == 0 else send(block, section, section, shift))
            return gather_dp(parts, 1)

        def own_row_block(value):
            return lax.dynamic_slice_in_dim(value, dp_id * own_rows, own_rows, 0)

        last = section_count - 1
        state = gather_dp(dp_all(tokens, 0, 0), 0)
        cot_full = gather_dp(dp_all(cotangent, last, last), 0)
        kept = []
        out_rows = [None] * section_count
        for k in range(section_count):
            wide = state.astype(F32)
            squares = sum_tensor(jnp.sum(wide * wide, axis=1)[None, :], k)
            scaled = (wide * gain_row[None, :]).astype(BF16)
            low_part = narrow(
                lax.dot_general(scaled, down_flat, (((1,), (1,)), ((), ())), preferred_element_type=F32)
            )
            low_raw = sum_tensor(low_part, k)
            product = jnp.dot(scaled, w_flat, preferred_element_type=F32).astype(BF16)
            blocks = product.reshape(rows, tensor_count, piece_cols)
            base = jnp.zeros((rows, piece_cols), F32)
            for shift in range(tensor_count):
                block = lax.dynamic_index_in_dim(
                    blocks, (tensor_id + shift) % tensor_count, 1, keepdims=False
                )
                if shift:
                    block = send(block, k, k, 0, shift)
                base = base + block.astype(F32)
            inverse = lax.rsqrt(squares / model_width + EPS)
            low = (low_raw * inverse).astype(BF16).T
            inverse = inverse[0]
            branch = base * inverse[:, None] + ADAPTER_SCALE * jnp.dot(
                spread(low), up_cols, preferred_element_type=F32
            )
            state_cols = own_cols(state).astype(F32)
            new_cols = (state_cols + branch).astype(BF16)
            kept.append((state, inverse, low, branch, state_cols))
            if k < last:
                state = gather_dp(dp_all(new_cols, k, k + 1), 1)
                out_rows[k] = send(own_row_block(state), k + 1, k)
            else:
                out_rows[k] = rows_from_cols(new_cols, k)
        grad_rows = [None] * section_count
        finals = [None] * section_count
        grad_cols = own_cols(cot_full)
        grad_parts = [grad_cols] + [send(grad_cols, last, last, 0, s) for s in range(1, tensor_count)]
        for k in range(last, -1, -1):
            state, inverse, low, branch, state_cols = kept[k]
            grad_cols = grad_parts[0]
            grad_wide = grad_cols.astype(F32)
            low_part = narrow(
                lax.dot_general(grad_cols, up_cols, (((1,), (1,)), ((), ())), preferred_element_type=F32)
            )
            stat_part = jnp.sum(grad_wide * branch, axis=1)
            small = sum_dp(sum_tensor(jnp.concatenate([low_part, stat_part[None, :]], axis=0), k), k)
            incoming = gather_tensor(grad_parts)
            partial = lax.dot_general(
                incoming, w_flat, (((1,), (1,)), ((), ())), preferred_element_type=F32
            ).astype(BF16)
            frozen = jnp.zeros((rows, piece_cols), F32)
            for shift in range(dp_count):
                at = ((dp_id + shift) % dp_count) * piece_cols
                block = lax.dynamic_slice_in_dim(partial, at, piece_cols, 1)
                if shift:
                    block = send(block, k, k, shift)
                frozen = frozen + block.astype(F32)
            if k == last:
                grad_full = cot_full
            else:
                grad_full = gather_dp(dp_all(grad_cols, k, k), 1)
                grad_rows[k + 1] = send(own_row_block(grad_full), k, k + 1)
            low_grad = small[:rank].astype(BF16).T
            statistic = small[rank]
            dnormed = frozen + ADAPTER_SCALE * jnp.dot(
                spread(low_grad), down_cols, preferred_element_type=F32
            )
            change = (
                grad_wide
                + inverse[:, None] * gain_cols[None, :] * dnormed
                - state_cols * (inverse * inverse * statistic / model_width)[:, None]
            )
            new_grad = change.astype(BF16)
            finals[k] = (state, inverse, low, low_grad, grad_full)
            if k > 0:
                grad_parts = [send(new_grad, k, k - 1, 0, s) for s in range(tensor_count)]
            else:
                grad_rows[0] = rows_from_cols(new_grad, 0)

        def mine(values):
            picked = values[0]
            for k in range(1, section_count):
                picked = jnp.where(section_id == k, values[k], picked)
            return picked

        state, inverse, low, low_grad, grad_full = [mine(list(v)) for v in zip(*finals)]
        normed = (state.astype(F32) * inverse[:, None] * gain_row[None, :]).astype(BF16)
        lanes = own_slots * rank

        def own_lanes(values):
            return lax.dynamic_slice_in_dim(spread(values), first_lane, lanes, 1)

        def adapter_grad(left, right):
            total = ADAPTER_SCALE * lax.dot_general(
                own_lanes(left), right, (((0,), (0,)), ((), ())), preferred_element_type=F32
            )
            return total.reshape(1, own_slots, rank, width_local)

        grad_a = adapter_grad(low_grad, normed)
        grad_b = adapter_grad(low, grad_full)
        return mine(out_rows)[None], mine(grad_rows)[None], grad_a, grad_b

    return local


def solution(mesh):
    placed = (
        P("dp", "tensor"),
        P("pipe", "tensor", None, "dp"),
        P("pipe", "tensor"),
        P("pipe", None, None, "tensor"),
        P("pipe", None, None, "tensor"),
        P("dp", "tensor"),
        P("dp"),
        P(),
    )
    return jax.shard_map(
        make_local(mesh.shape["pipe"], mesh.shape["dp"], mesh.shape["tensor"]),
        mesh=mesh,
        in_specs=placed,
        out_specs=(
            P("pipe", "dp", "tensor"),
            P("pipe", "dp", "tensor"),
            P("pipe", "dp", None, "tensor"),
            P("pipe", "dp", None, "tensor"),
        ),
        check_vma=False,
    )
```

```python
import jax
import jax.numpy as jnp
from jax import lax
from jax.sharding import PartitionSpec as P

EPS = 1e-05
ADAPTER_SCALE = 2.0
F32 = jnp.float32
BF16 = jnp.bfloat16


def make_local(section_count, dp_count, tensor_count):
    axes = ("pipe", "dp", "tensor")

    def index_of(section, dp, tensor):
        return (section * dp_count + dp) * tensor_count + tensor

    def send(value, source, target, dp_shift=0, tensor_shift=0):
        pairs = [
            (
                index_of(source, d, t),
                index_of(target, (d + dp_shift) % dp_count, (t + tensor_shift) % tensor_count),
            )
            for d in range(dp_count)
            for t in range(tensor_count)
        ]
        return lax.ppermute(value, axes, pairs)

    def local(tokens, weight, gain, resident_down, resident_up, cotangent, batch_tenants, tenant_slots):
        section_id = lax.axis_index("pipe")
        dp_id = lax.axis_index("dp")
        tensor_id = lax.axis_index("tensor")
        w_block = weight[0]
        gain_row = gain[0]
        width_local, _, piece_cols = w_block.shape
        w_flat = w_block.reshape(width_local, tensor_count * piece_cols)
        model_width = width_local * tensor_count
        own_rows = tokens.shape[0]
        rows = own_rows * dp_count
        slots, rank = resident_down.shape[1:3]
        micro_rows = own_rows // batch_tenants.shape[0]
        own_slots = slots // dp_count
        down_flat = resident_down[0].reshape(slots * rank, width_local)
        up_flat = resident_up[0].reshape(slots * rank, width_local)
        first_col = dp_id * piece_cols

        def gather_dp(parts_by_shift, axis):
            stacked = jnp.stack(parts_by_shift)
            order = [
                lax.dynamic_index_in_dim(stacked, (dp_id - d) % dp_count, 0, keepdims=False)
                for d in range(dp_count)
            ]
            return jnp.concatenate(order, axis=axis)

        def own_cols(array):
            return lax.dynamic_slice_in_dim(array, first_col, piece_cols, array.ndim - 1)

        down_cols = own_cols(down_flat)
        up_cols = own_cols(up_flat)
        gain_cols = own_cols(gain_row)
        tenant_parts = [batch_tenants] + [
            lax.ppermute(batch_tenants, "dp", [(d, (d + s) % dp_count) for d in range(dp_count)])
            for s in range(1, dp_count)
        ]
        all_tenants = gather_dp(tenant_parts, 0)
        labels = jnp.arange(slots, dtype=jnp.int32)
        slot_ids = jnp.sum(
            jnp.where(all_tenants[:, None] == labels[None, :], tenant_slots[None, :], 0), axis=1
        )
        row_slots = jnp.repeat(slot_ids, micro_rows)
        picks = row_slots[:, None] == labels[None, :]
        lane_slot = jnp.arange(slots * rank, dtype=jnp.int32) // rank
        lane_rank = jnp.arange(slots * rank, dtype=jnp.int32) % rank
        lane_pick = row_slots[:, None] == lane_slot[None, :]
        fold = (lane_rank[:, None] == jnp.arange(rank)[None, :]).astype(F32)
        first_lane = dp_id * own_slots * rank

        def narrow(terms):
            kept = jnp.where(lane_pick, terms, 0.0).reshape(rows, slots, rank)
            return jnp.sum(kept, axis=1).T

        def spread(values):
            wide = jnp.tile(values, (1, slots))
            return jnp.where(lane_pick, wide, jnp.zeros((), values.dtype))

        def gather_tensor(parts_by_shift):
            stacked = jnp.stack(parts_by_shift)
            order = [
                lax.dynamic_index_in_dim(stacked, (tensor_id - t) % tensor_count, 0, keepdims=False)
                for t in range(tensor_count)
            ]
            return jnp.concatenate(order, axis=1)

        def sum_tensor(value, section):
            total = value
            for shift in range(1, tensor_count):
                total = total + send(value, section, section, 0, shift)
            return total

        def sum_dp(value, section):
            total = value
            for shift in range(1, dp_count):
                total = total + send(value, section, section, shift, 0)
            return total

        def dp_all(value, source, target):
            head = value if source == target else send(value, source, target)
            return [head] + [send(value, source, target, s) for s in range(1, dp_count)]

        def rows_from_cols(value, section):
            parts = []
            for shift in range(dp_count):
                at = ((dp_id + shift) % dp_count) * own_rows
                block = lax.dynamic_slice_in_dim(value, at, own_rows, 0)
                parts.append(block if shift == 0 else send(block, section, section, shift))
            return gather_dp(parts, 1)

        def own_row_block(value):
            return lax.dynamic_slice_in_dim(value, dp_id * own_rows, own_rows, 0)

        last = section_count - 1
        state = gather_dp(dp_all(tokens, 0, 0), 0)
        cot_full = gather_dp(dp_all(cotangent, last, last), 0)
        kept = []
        out_rows = [None] * section_count
        for k in range(section_count):
            wide = state.astype(F32)
            squares = sum_tensor(jnp.sum(wide * wide, axis=1)[None, :], k)
            scaled = (wide * gain_row[None, :]).astype(BF16)

            def project(values):
                low = lax.dot_general(
                    values, down_flat, (((1,), (1,)), ((), ())), preferred_element_type=F32
                )
                return jnp.dot(values, w_flat, preferred_element_type=F32).astype(BF16), low

            def skipped(values):
                return (
                    jnp.zeros((rows, tensor_count * piece_cols), BF16),
                    jnp.zeros((rows, slots * rank), F32),
                )

            product, all_terms = lax.cond(section_id == k, project, skipped, scaled)
            low_raw = sum_tensor(narrow(all_terms), k)
            blocks = product.reshape(rows, tensor_count, piece_cols)
            base = jnp.zeros((rows, piece_cols), F32)
            for shift in range(tensor_count):
                block = lax.dynamic_index_in_dim(
                    blocks, (tensor_id + shift) % tensor_count, 1, keepdims=False
                )
                if shift:
                    block = send(block, k, k, 0, shift)
                base = base + block.astype(F32)
            inverse = lax.rsqrt(squares / model_width + EPS)
            low = (low_raw * inverse).astype(BF16).T
            inverse = inverse[0]
            branch = base * inverse[:, None] + ADAPTER_SCALE * jnp.dot(
                spread(low), up_cols, preferred_element_type=F32
            )
            state_cols = own_cols(state).astype(F32)
            new_cols = (state_cols + branch).astype(BF16)
            kept.append((state, inverse, low, branch, state_cols))
            if k < last:
                state = gather_dp(dp_all(new_cols, k, k + 1), 1)
                out_rows[k] = send(own_row_block(state), k + 1, k)
            else:
                out_rows[k] = rows_from_cols(new_cols, k)
        grad_rows = [None] * section_count
        finals = [None] * section_count
        grad_cols = own_cols(cot_full)
        grad_parts = [grad_cols] + [send(grad_cols, last, last, 0, s) for s in range(1, tensor_count)]
        for k in range(last, -1, -1):
            state, inverse, low, branch, state_cols = kept[k]
            grad_cols = grad_parts[0]
            grad_wide = grad_cols.astype(F32)
            low_part = narrow(
                lax.dot_general(grad_cols, up_cols, (((1,), (1,)), ((), ())), preferred_element_type=F32)
            )
            stat_part = jnp.sum(grad_wide * branch, axis=1)
            small = sum_dp(sum_tensor(jnp.concatenate([low_part, stat_part[None, :]], axis=0), k), k)
            incoming = gather_tensor(grad_parts)
            if k == last:
                grad_full = cot_full
            else:
                grad_full = gather_dp(dp_all(grad_cols, k, k), 1)

            def back(values):
                return lax.dot_general(
                    values, w_flat, (((1,), (1,)), ((), ())), preferred_element_type=F32
                ).astype(BF16)

            def back_skipped(values):
                return jnp.zeros((rows, width_local), BF16)

            partial = lax.cond(section_id == k, back, back_skipped, incoming)
            partial, grad_full = lax.optimization_barrier((partial, grad_full))
            frozen = jnp.zeros((rows, piece_cols), F32)
            for shift in range(dp_count):
                at = ((dp_id + shift) % dp_count) * piece_cols
                block = lax.dynamic_slice_in_dim(partial, at, piece_cols, 1)
                if shift:
                    block = send(block, k, k, shift)
                frozen = frozen + block.astype(F32)
            if k < last:
                grad_rows[k + 1] = send(own_row_block(grad_full), k, k + 1)
            low_grad = small[:rank].astype(BF16).T
            statistic = small[rank]
            dnormed = frozen + ADAPTER_SCALE * jnp.dot(
                spread(low_grad), down_cols, preferred_element_type=F32
            )
            change = (
                grad_wide
                + inverse[:, None] * gain_cols[None, :] * dnormed
                - state_cols * (inverse * inverse * statistic / model_width)[:, None]
            )
            new_grad = change.astype(BF16)
            finals[k] = (state, inverse, low, low_grad, grad_full)
            if k > 0:
                grad_parts = [send(new_grad, k, k - 1, 0, s) for s in range(tensor_count)]
            else:
                grad_rows[0] = rows_from_cols(new_grad, 0)

        def mine(values):
            picked = values[0]
            for k in range(1, section_count):
                picked = jnp.where(section_id == k, values[k], picked)
            return picked

        state, inverse, low, low_grad, grad_full = [mine(list(v)) for v in zip(*finals)]
        normed = (state.astype(F32) * inverse[:, None] * gain_row[None, :]).astype(BF16)
        lanes = own_slots * rank

        def own_lanes(values):
            return lax.dynamic_slice_in_dim(spread(values), first_lane, lanes, 1)

        def adapter_grad(left, right):
            total = ADAPTER_SCALE * lax.dot_general(
                own_lanes(left), right, (((0,), (0,)), ((), ())), preferred_element_type=F32
            )
            return total.reshape(1, own_slots, rank, width_local)

        grad_a = adapter_grad(low_grad, normed)
        grad_b = adapter_grad(low, grad_full)
        return mine(out_rows)[None], mine(grad_rows)[None], grad_a, grad_b

    return local


def solution(mesh):
    placed = (
        P("dp", "tensor"),
        P("pipe", "tensor", None, "dp"),
        P("pipe", "tensor"),
        P("pipe", None, None, "tensor"),
        P("pipe", None, None, "tensor"),
        P("dp", "tensor"),
        P("dp"),
        P(),
    )
    return jax.shard_map(
        make_local(mesh.shape["pipe"], mesh.shape["dp"], mesh.shape["tensor"]),
        mesh=mesh,
        in_specs=placed,
        out_specs=(
            P("pipe", "dp", "tensor"),
            P("pipe", "dp", "tensor"),
            P("pipe", "dp", None, "tensor"),
            P("pipe", "dp", None, "tensor"),
        ),
        check_vma=False,
    )
```
